256 devices in a mesh: dom: 32 (over x_hi, z, core), ka: 8 (over x_lo, y).
Axes of the slice: x: 4 (x_hi: 2, x_lo: 2; x = x_hi * 2 + x_lo), y: 4, z: 8, core: 2. Of those that a mesh axis runs over, the one named last changes fastest.
Arguments:
- frac: float32 [3, 131072], P(None, 'dom'), may hold values from 0 to 1
- species: int32 [131072], P('dom'), may hold values from 0 to 7
- feats: bfloat16 [131072, 256], P('dom'), may hold values from -6 to 6
- cotangent: bfloat16 [131072, 256], P('dom'), may hold values from -6 to 6
- miller: int32 [3, 2048], P(None, 'ka'), may hold values from -8 to 8, as said below
- species_gain: float32 [8, 256], replicated, may hold values from 0.1 to 1.9
- filter_weight: float32 [16, 256], replicated, may hold values from -4 to 4
Outputs:
- updated: bfloat16 [131072, 256], P('dom')
- forces: float32 [3, 131072], P(None, 'dom')
The draws below stay inside these ranges and needn't reach their ends.
Inputs may be any that keep to these rules, and one draw needn't show every extreme that they name: `miller`: no k-vector has all three indices zero; both -8 and 8 occur.
All inputs are finite; a program needn't handle non-finite values.
Results may differ from the reference program's by a relative error of at most 0.006.
Values may be sent and summed in bfloat16 or wider, within the bound.
No kernel may reach another device: no remote copies, remote signals or barrier semaphores. Data moves between devices by JAX's collectives and lax.ppermute only.
A program may use at most 64 MiB of HBM per device.

```python
import math
import jax
import jax.numpy as jnp
from jax import lax

CH = 256
K = 2048
NB = 16
SPECIES = 8
MILLER = 8
ATOM_DEV = 4096
ATOMS = 131072
N_DOM = 32


def draw_miller(key, part):
    key = jax.random.fold_in(key, 7)
    values = jax.random.randint(key, (3, K), -MILLER, MILLER + 1)
    empty = jnp.all(values == 0, axis=0)
    values = values.at[0].set(jnp.where(empty, 1, values[0]))
    values = values.at[0, 0].set(MILLER)
    values = values.at[1, 0].set(-MILLER)
    return values.astype(jnp.int32)


def set_ends(entries, stream_key, smallest, high):
    index_at = [jax.random.randint(jax.random.fold_in(stream_key, axis), (), 0, length) for axis, length in enumerate(entries.shape)]
    main_axis = entries.shape.index(max(entries.shape))
    next_to = index_at[:main_axis] + [(index_at[main_axis] + 1) % entries.shape[main_axis]] + index_at[main_axis + 1:]
    return entries.at[tuple(index_at)].set(smallest).at[tuple(next_to)].set(high)


def steps_of(rng, dims, pieces, low, high):
    loudness = 1.0
    for position, shards_of in pieces:
        heights = jax.random.uniform(jax.random.fold_in(jax.random.fold_in(rng, 6), position), (shards_of,), jnp.float32, low / len(pieces), high / len(pieces))
        loudness = loudness * jnp.repeat(jnp.exp(heights), dims[position] // shards_of).reshape((-1,) + (1,) * (len(dims) - 1 - position))
    return loudness


def gaussian(stream_key, dims, scale, reach, pieces=(), kind=jnp.bfloat16):
    gain = steps_of(stream_key, dims, pieces, -0.22, 0.18) if pieces else 1.0
    drawn = jax.random.normal(stream_key, dims, jnp.float32) * scale * gain
    return jnp.minimum(jnp.maximum(drawn, -reach), reach).astype(kind)


def setup_inputs(seed: int = 0) -> dict:
    streams_of = jax.random.split(jax.random.key(seed), 8)
    return {
        "frac": jnp.clip(1.0 * jax.random.uniform(streams_of[0], (3, ATOMS), jnp.float32) ** steps_of(streams_of[0], (3, ATOMS), ((1, 32),), -0.2, 0.2), 0.0, 1.0),
        "species": set_ends(jax.random.randint(streams_of[1], (ATOMS,), 0, SPECIES), jax.random.fold_in(streams_of[1], 1), 0, SPECIES - 1).astype(jnp.int32),
        "feats": gaussian(streams_of[2], (ATOMS, CH), 1.0, 6.0, ((0, 32),)),
        "cotangent": gaussian(streams_of[3], (ATOMS, CH), 1.0, 6.0, ((0, 32),)),
        "miller": draw_miller(jax.random.fold_in(streams_of[7], 71), 0),
        "species_gain": jnp.clip(1.0 + 0.18 * jax.random.normal(streams_of[5], (SPECIES, CH), jnp.float32), 0.1, 1.9),
        "filter_weight": gaussian(streams_of[6], (NB, CH), 1.0, 4.0, (), jnp.float32),
    }


TWO_PI = 6.283185307179586
BOX = 64.0

def phase_tables(frac, miller):
    theta = TWO_PI * lax.dot_general(frac, miller.astype(jnp.float32), (((0,), (0,)), ((), ())), precision=lax.Precision.HIGHEST)
    return (jnp.cos(theta).astype(jnp.bfloat16), jnp.sin(theta).astype(jnp.bfloat16))

def kernel_weights(miller, filter_weight):
    mills = miller.astype(jnp.float32)
    length = jnp.sqrt(lax.optimization_barrier(jnp.sum(mills * mills, axis=0)))
    count = filter_weight.shape[0]
    centres = jnp.arange(count, dtype=jnp.float32) * (14.0 / (count - 1))
    basis = jnp.exp(-(length[:, None] - centres[None, :]) ** 2)
    return jnp.dot(basis, filter_weight, precision=lax.Precision.HIGHEST)

def species_rows(feats, species, species_gain):
    onehot = (species[:, None] == jnp.arange(species_gain.shape[0], dtype=jnp.int32)[None, :]).astype(jnp.float32)
    gains = jnp.dot(onehot, species_gain, precision=lax.Precision.HIGHEST)
    return (feats.astype(jnp.float32) * gains).astype(jnp.bfloat16)

def project(table, rows):
    return lax.dot_general(table, rows, (((0,), (0,)), ((), ())), preferred_element_type=jnp.float32)

def against(left, panel):
    return lax.dot_general(left, panel, (((1,), (1,)), ((), ())), preferred_element_type=jnp.float32)

def angle_grad(cos_t, sin_t, cotangent, embedded, panels, inv_k, inv_n):
    fr, fi, ar, ai = panels
    cosf = cos_t.astype(jnp.float32)
    sinf = sin_t.astype(jnp.float32)
    direct = -sinf * against(cotangent, fr) + cosf * against(cotangent, fi)
    through = -sinf * against(embedded, ar) + cosf * against(embedded, ai)
    return direct * inv_k + through * inv_n

def force_terms(miller, grads):
    return -TWO_PI / BOX * lax.dot_general(miller.astype(jnp.float32), grads, (((1,), (1,)), ((), ())), precision=lax.Precision.HIGHEST)

def reference(frac, species, feats, cotangent, miller, species_gain, filter_weight):
    inv_n = 1.0 / math.sqrt(ATOMS)
    inv_k = 1.0 / math.sqrt(K)
    frac_b = frac.reshape(3, N_DOM, ATOM_DEV).transpose(1, 0, 2)
    spec_b = species.reshape(N_DOM, ATOM_DEV)
    feat_b = feats.reshape(N_DOM, ATOM_DEV, CH)
    cot_b = cotangent.reshape(N_DOM, ATOM_DEV, CH)
    weights = kernel_weights(miller, filter_weight)

    def accumulate(carry, block):
        frac_blk, spec_blk, feat_blk, cot_blk = block
        cos_t, sin_t = phase_tables(frac_blk, miller)
        embedded = species_rows(feat_blk, spec_blk, species_gain)
        terms = (project(cos_t, embedded), project(sin_t, embedded), project(cos_t, cot_blk), project(sin_t, cot_blk))
        return (tuple((c + t for c, t in zip(carry, terms))), None)
    zero = jnp.zeros((K, CH), jnp.float32)
    sums, _ = lax.scan(accumulate, (zero, zero, zero, zero), (frac_b, spec_b, feat_b, cot_b))
    sr, si, gr, gi = sums
    fr = (weights * sr * inv_n).astype(jnp.bfloat16)
    fi = (weights * si * inv_n).astype(jnp.bfloat16)
    ar = (weights * gr * inv_k).astype(jnp.bfloat16)
    ai = (weights * gi * inv_k).astype(jnp.bfloat16)

    def finish(block):
        frac_blk, spec_blk, feat_blk, cot_blk = block
        cos_t, sin_t = phase_tables(frac_blk, miller)
        embedded = species_rows(feat_blk, spec_blk, species_gain)
        message = jnp.dot(cos_t, fr, preferred_element_type=jnp.float32) + jnp.dot(sin_t, fi, preferred_element_type=jnp.float32)
        updated = (feat_blk.astype(jnp.float32) + message * inv_k).astype(jnp.bfloat16)
        grads = angle_grad(cos_t, sin_t, cot_blk, embedded, (fr, fi, ar, ai), inv_k, inv_n)
        return (updated, force_terms(miller, grads))
    updated_b, force_b = lax.map(finish, (frac_b, spec_b, feat_b, cot_b))
    return (updated_b.reshape(ATOMS, CH), force_b.transpose(1, 0, 2).reshape(3, ATOMS))
```

```python
import functools
import math

import jax
import jax.numpy as jnp
from jax import lax
from jax.experimental import pallas as pl
from jax.experimental.pallas import tpu as pltpu
from jax.sharding import Mesh, PartitionSpec as P

TWO_PI = 6.283185307179586
BOX = 64.0
MIB = 1024 * 1024
SINE = (4.4428679, -7.30744342, 3.59478803, -0.7843739)
COSINE = (1.41420408, -6.97764207, 5.71523842, -1.72834863)
OVER = ("xh", "z")
ACROSS = ("xl", "y")
SWAP = [(0, 1), (1, 0)]


def triple(x):
    hi = x.astype(jnp.bfloat16)
    rest = x - hi.astype(jnp.float32)
    mid = rest.astype(jnp.bfloat16)
    low = (rest - mid.astype(jnp.float32)).astype(jnp.bfloat16)
    return jnp.concatenate([hi, mid, low], axis=0)


def contract(left, right, dims):
    return lax.dot_general(left, right, (dims, ((), ())), preferred_element_type=jnp.float32)


def cos_sin(turns):
    r = turns - jnp.round(turns)
    t = r * r
    s = (((SINE[3] * t + SINE[2]) * t + SINE[1]) * t + SINE[0]) * r
    c = ((COSINE[3] * t + COSINE[2]) * t + COSINE[1]) * t + COSINE[0]
    return 1.0 - s * s, s * c


def factors_kernel(frac, species, feats, cot, miller, gain, emb, tab, part, acc, turns):
    step = pl.program_id(0)
    kn = miller.shape[1]
    mill = miller[...].astype(jnp.float32).astype(jnp.bfloat16)
    mill3 = jnp.concatenate([mill, mill, mill], axis=0)
    turns[...] = contract(mill3, triple(frac[...]), ((0,), (0,)))
    kinds = gain.shape[0]
    onehot = (lax.broadcasted_iota(jnp.int32, (kinds, species.shape[1]), 0) == species[...]).astype(jnp.float32)
    onehot = onehot.astype(jnp.bfloat16)
    onehot3 = jnp.concatenate([onehot, onehot, onehot], axis=0)
    gains = contract(onehot3, triple(gain[...]), ((0,), (0,)))
    rows = (feats[...].astype(jnp.float32) * gains).astype(jnp.bfloat16)
    emb[...] = rows

    def chunk(i, _):
        at = pl.ds(pl.multiple_of(i * 16, 16), 16)
        c, s = cos_sin(turns[at, :])
        tab[at, :] = c.astype(jnp.bfloat16)
        tab[pl.ds(pl.multiple_of(kn + i * 16, 16), 16), :] = s.astype(jnp.bfloat16)
        return 0

    lax.fori_loop(0, kn // 16, chunk, 0, unroll=4)

    @pl.when(step == 0)
    def _():
        acc[...] = jnp.zeros_like(acc)

    both = jnp.concatenate([rows, cot[...]], axis=1)
    acc[...] += contract(tab[...], both, ((1,), (0,)))

    @pl.when(step == pl.num_programs(0) - 1)
    def _():
        part[...] = acc[...].astype(jnp.bfloat16)


def factors(frac, species, feats, cot, miller, gain, tile=512):
    n, ch = feats.shape
    kn = miller.shape[1]
    return pl.pallas_call(
        factors_kernel,
        grid=(n // tile,),
        in_specs=[
            pl.BlockSpec((3, tile), lambda i: (0, i)),
            pl.BlockSpec((1, tile), lambda i: (0, i)),
            pl.BlockSpec((tile, ch), lambda i: (i, 0)),
            pl.BlockSpec((tile, ch), lambda i: (i, 0)),
            pl.BlockSpec((3, kn), lambda i: (0, 0)),
            pl.BlockSpec(gain.shape, lambda i: (0, 0)),
        ],
        out_specs=[
            pl.BlockSpec((tile, ch), lambda i: (i, 0)),
            pl.BlockSpec((2 * kn, tile), lambda i: (0, i)),
            pl.BlockSpec((2 * kn, 2 * ch), lambda i: (0, 0)),
        ],
        out_shape=[
            jax.ShapeDtypeStruct((n, ch), jnp.bfloat16),
            jax.ShapeDtypeStruct((2 * kn, n), jnp.bfloat16),
            jax.ShapeDtypeStruct((2 * kn, 2 * ch), jnp.bfloat16),
        ],
        scratch_shapes=[
            pltpu.VMEM((2 * kn, 2 * ch), jnp.float32),
            pltpu.VMEM((kn, tile), jnp.float32),
        ],
        compiler_params=pltpu.CompilerParams(vmem_limit_bytes=16 * MIB),
        cost_estimate=pl.CostEstimate(flops=8 * n * kn * ch, bytes_accessed=8 * n * ch + 4 * n * kn, transcendentals=0),
        name="factors",
    )(frac, species, feats, cot, miller, gain)


def tables_kernel(frac, mill, cos, sin, turns):
    turns[...] = contract(triple(frac[...]), mill[...], ((0,), (0,)))

    def chunk(i, _):
        at = pl.ds(pl.multiple_of(i * 16, 16), 16)
        c, s = cos_sin(turns[at, :])
        cos[at, :] = c.astype(jnp.bfloat16)
        sin[at, :] = s.astype(jnp.bfloat16)
        return 0

    lax.fori_loop(0, turns.shape[0] // 16, chunk, 0, unroll=4)


def tables(frac, mill, tile=512, wide=512):
    n = frac.shape[1]
    kn = mill.shape[1]
    return pl.pallas_call(
        tables_kernel,
        grid=(n // tile, kn // wide),
        in_specs=[
            pl.BlockSpec((3, tile), lambda i, j: (0, i)),
            pl.BlockSpec((mill.shape[0], wide), lambda i, j: (0, j)),
        ],
        out_specs=[pl.BlockSpec((tile, wide), lambda i, j: (i, j))] * 2,
        out_shape=[jax.ShapeDtypeStruct((n, kn), jnp.bfloat16)] * 2,
        scratch_shapes=[pltpu.VMEM((tile, wide), jnp.float32)],
        compiler_params=pltpu.CompilerParams(vmem_limit_bytes=8 * MIB),
        cost_estimate=pl.CostEstimate(flops=20 * n * kn * 200, bytes_accessed=4 * n * kn, transcendentals=0),
        name="tables",
    )(frac, mill)


def forces_kernel(scale, tab, cot, emb, panel, mill, out, work):
    kn = mill.shape[0]
    both = jnp.concatenate([cot[...], emb[...]], axis=1)
    work[...] = contract(panel[...], both, ((1,), (1,)))

    def chunk(i, sums):
        at = pl.ds(pl.multiple_of(i * 16, 16), 16)
        at2 = pl.ds(pl.multiple_of(kn + i * 16, 16), 16)
        c = tab[at, :].astype(jnp.float32)
        s = tab[at2, :].astype(jnp.float32)
        grads = c * work[at2, :] - s * work[at, :]
        m = mill[at, :]
        return tuple(total + m[:, d:d + 1] * grads for d, total in enumerate(sums))

    zero = jnp.zeros((16, tab.shape[1]), jnp.float32)
    sums = lax.fori_loop(0, kn // 16, chunk, (zero, zero, zero), unroll=2)
    out[...] = jnp.concatenate([jnp.sum(total, axis=0, keepdims=True) for total in sums], axis=0) * scale


def forces_of(tab, cot, emb, panel, mill, scale, tile=512):
    n, ch = cot.shape
    kn = mill.shape[0]
    return pl.pallas_call(
        functools.partial(forces_kernel, scale),
        grid=(n // tile,),
        in_specs=[
            pl.BlockSpec((2 * kn, tile), lambda i: (0, i)),
            pl.BlockSpec((tile, ch), lambda i: (i, 0)),
            pl.BlockSpec((tile, ch), lambda i: (i, 0)),
            pl.BlockSpec((2 * kn, 2 * ch), lambda i: (0, 0)),
            pl.BlockSpec(mill.shape, lambda i: (0, 0)),
        ],
        out_specs=pl.BlockSpec((3, tile), lambda i: (0, i)),
        out_shape=jax.ShapeDtypeStruct((3, n), jnp.float32),
        scratch_shapes=[pltpu.VMEM((2 * kn, tile), jnp.float32)],
        compiler_params=pltpu.CompilerParams(vmem_limit_bytes=16 * MIB),
        cost_estimate=pl.CostEstimate(flops=8 * n * kn * ch, bytes_accessed=4 * n * kn + 4 * n * ch, transcendentals=0),
        name="forces",
    )(tab, cot, emb, panel, mill)


def message_kernel(scale, cos, sin, real, imag, feats, out):
    total = contract(cos[...], real[...], ((1,), (0,))) + contract(sin[...], imag[...], ((1,), (0,)))
    out[...] = (feats[...].astype(jnp.float32) + total * scale).astype(jnp.bfloat16)


def message(cos, sin, real, imag, feats, scale, tile=512):
    n, ch = feats.shape
    kn = real.shape[0]
    return pl.pallas_call(
        functools.partial(message_kernel, scale),
        grid=(n // tile,),
        in_specs=[
            pl.BlockSpec((tile, kn), lambda i: (i, 0)),
            pl.BlockSpec((tile, kn), lambda i: (i, 0)),
            pl.BlockSpec((kn, ch), lambda i: (0, 0)),
            pl.BlockSpec((kn, ch), lambda i: (0, 0)),
            pl.BlockSpec((tile, ch), lambda i: (i, 0)),
        ],
        out_specs=pl.BlockSpec((tile, ch), lambda i: (i, 0)),
        out_shape=jax.ShapeDtypeStruct((n, ch), jnp.bfloat16),
        compiler_params=pltpu.CompilerParams(vmem_limit_bytes=24 * MIB),
        cost_estimate=pl.CostEstimate(flops=4 * n * kn * ch, bytes_accessed=4 * n * kn + 4 * n * ch, transcendentals=0),
        name="message",
    )(cos, sin, real, imag, feats)


def weights_of(mills, filter_weight):
    length = jnp.sqrt(jnp.sum(mills * mills, axis=0))
    count = filter_weight.shape[0]
    centres = jnp.arange(count, dtype=jnp.float32) * (14.0 / (count - 1))
    basis = jnp.exp(-((length[:, None] - centres[None, :]) ** 2))
    return jnp.dot(basis, filter_weight, precision=lax.Precision.HIGHEST)


def everyone(x, axes):
    n = lax.axis_size(axes)
    return lax.all_to_all(jnp.broadcast_to(x[None], (n,) + x.shape), axes, 0, 0)


def body(frac, species, feats, cot, miller, gain, filter_weight):
    n, ch = feats.shape
    kn = miller.shape[1]
    inv_n = 1.0 / math.sqrt(n * lax.axis_size(("xh", "z", "core")))
    inv_k = 1.0 / math.sqrt(kn * lax.axis_size(ACROSS))
    groups = lax.axis_size(OVER)
    rows = kn // groups
    core = lax.axis_index("core")

    mills = miller.astype(jnp.float32)
    mill_all = everyone(jnp.concatenate([mills] * 3, axis=0).astype(jnp.bfloat16), ACROSS)
    mill_all = mill_all.transpose(1, 0, 2).reshape(9, -1)

    emb, tab, part = factors(frac, species.reshape(1, n), feats, cot, miller, gain)
    cos, sin = tables(frac, mill_all)

    mine = lax.dynamic_slice_in_dim(mills, lax.axis_index(OVER) * rows, rows, axis=1)
    weights = weights_of(mine, filter_weight) * inv_n

    halves = part.reshape(2, kn, 2 * ch)
    keep = lax.dynamic_index_in_dim(halves, core, 0, keepdims=False)
    give = lax.dynamic_index_in_dim(halves, 1 - core, 0, keepdims=False)
    got = lax.ppermute(give, "core", SWAP)
    pair = (keep.astype(jnp.float32) + got.astype(jnp.float32)).astype(jnp.bfloat16)
    spread = lax.all_to_all(pair.reshape(groups, rows, 2 * ch), OVER, 0, 0)
    total = jnp.sum(spread.astype(jnp.float32), axis=0)
    panel = (total * jnp.concatenate([weights, weights], axis=1)).astype(jnp.bfloat16)
    panel = everyone(panel, OVER).reshape(kn, 2 * ch)

    everywhere = everyone(panel[:, :ch], ACROSS).reshape(-1, ch)
    other = lax.ppermute(panel, "core", SWAP)
    first = core == 0
    local = jnp.concatenate([jnp.where(first, panel, other), jnp.where(first, other, panel)], axis=0)
    force = forces_of(tab, cot, emb, local, mills.T, -TWO_PI / BOX * inv_k)
    force_all = everyone(force, ACROSS)
    forces = jnp.sum(force_all, axis=0)

    other = lax.ppermute(everywhere, "core", SWAP)
    real = jnp.where(first, everywhere, other)
    imag = jnp.where(first, other, everywhere)
    updated = message(cos, sin, real, imag, feats, inv_k)
    return updated, forces


def solution(mesh):
    sizes = dict(mesh.shape)
    fine = Mesh(mesh.devices.reshape(2, sizes["dom"] // 4, 2, 2, sizes["ka"] // 2), ("xh", "z", "core", "xl", "y"))
    dom = ("xh", "z", "core")
    placed = (P(None, dom), P(dom), P(dom, None), P(dom, None), P(None, ACROSS), P(), P())
    return jax.shard_map(
        body,
        mesh=fine,
        in_specs=placed,
        out_specs=(P(dom, None), P(None, dom)),
        check_vma=False,
    )
```

```python
import functools
import math

import jax
import jax.numpy as jnp
from jax import lax
from jax.experimental import pallas as pl
from jax.experimental.pallas import tpu as pltpu
from jax.sharding import Mesh, PartitionSpec as P

TWO_PI = 6.283185307179586
BOX = 64.0
MIB = 1024 * 1024
SINE = (4.4428679, -7.30744342, 3.59478803, -0.7843739)
COSINE = (1.41420408, -6.97764207, 5.71523842, -1.72834863)
OVER = ("xh", "z")
ACROSS = ("xl", "y")
SWAP = [(0, 1), (1, 0)]
DEPTH = 16
SHARED = 4
TILE = 512
WHOLE = pl.BlockSpec(memory_space=pltpu.VMEM)
SCALAR = pl.BlockSpec(memory_space=pltpu.SMEM)
FAR = pl.BlockSpec(memory_space=pltpu.HBM)


def triple(x):
    hi = x.astype(jnp.bfloat16)
    rest = x - hi.astype(jnp.float32)
    mid = rest.astype(jnp.bfloat16)
    low = (rest - mid.astype(jnp.float32)).astype(jnp.bfloat16)
    return [hi, mid, low]


def places(frac):
    n = frac.shape[1]
    rest = DEPTH - 10
    return jnp.concatenate(
        triple(frac) + [jnp.ones((1, n), jnp.bfloat16), jnp.zeros((rest, n), jnp.bfloat16)], axis=0
    )


def contract(left, right, dims):
    return lax.dot_general(left, right, (dims, ((), ())), preferred_element_type=jnp.float32)


def cos_sin(turns):
    r = turns - jnp.round(turns)
    t = r * r
    s = (((SINE[3] * t + SINE[2]) * t + SINE[1]) * t + SINE[0]) * r
    c = ((COSINE[3] * t + COSINE[2]) * t + COSINE[1]) * t + COSINE[0]
    return (1.0 - s * s).astype(jnp.bfloat16), (s * c).astype(jnp.bfloat16)


def params(mib):
    return pltpu.CompilerParams(vmem_limit_bytes=mib * MIB)


def cost(flops, moved):
    return pl.CostEstimate(flops=flops, bytes_accessed=moved, transcendentals=0)


def steps_of(miller, core):
    kn = miller.shape[1]
    mills = miller.astype(jnp.float32) * (1.0 - 2.0 * core)
    rows = [mills, mills, mills, jnp.full((1, kn), 0.25 * core), jnp.zeros((DEPTH - 10, kn), jnp.float32)]
    return jnp.concatenate(rows, axis=0).astype(jnp.bfloat16)


def prepare_kernel(scale, miller, filter_weight, weights, columns):
    kn = miller.shape[1]
    column = jnp.concatenate([miller[...].astype(jnp.float32), jnp.zeros((5, kn), jnp.float32)], axis=0).T
    columns[...] = column
    length = jnp.sqrt(jnp.sum(column * column, axis=1, keepdims=True))
    count = filter_weight.shape[0]
    centres = lax.broadcasted_iota(jnp.int32, (1, count), 1).astype(jnp.float32) * (14.0 / (count - 1))
    basis = jnp.exp(-((length - centres) ** 2))
    weights[...] = scale * jnp.dot(
        basis, filter_weight[...], precision=lax.Precision.HIGHEST, preferred_element_type=jnp.float32
    )


def prepare(miller, filter_weight, scale):
    kn = miller.shape[1]
    return pl.pallas_call(
        functools.partial(prepare_kernel, scale),
        in_specs=[WHOLE, WHOLE],
        out_specs=[WHOLE] * 2,
        out_shape=[
            jax.ShapeDtypeStruct((kn, filter_weight.shape[1]), jnp.float32),
            jax.ShapeDtypeStruct((kn, 8), jnp.float32),
        ],
        compiler_params=params(4),
        cost_estimate=cost(10**6, 10**5),
        name="prepare",
    )(miller, filter_weight)


def factors_kernel(tile, core, frac, species, feats, cot, miller, gain, emb, tab, keep, give, acc, held):
    n, ch = feats.shape
    kn = miller.shape[1]
    kinds = gain.shape[0]
    acc[...] = jnp.zeros_like(acc)
    held[...] = steps_of(miller[...], core[0]).T
    gains3 = jnp.concatenate(triple(gain[...]), axis=0)

    def part(frac, species, feats, cot, emb, tab):
        place = places(frac[...])
        onehot = (lax.broadcasted_iota(jnp.int32, (kinds, tile), 0) == species[...]).astype(jnp.float32)
        onehot = onehot.astype(jnp.bfloat16)
        gains = contract(jnp.concatenate([onehot, onehot, onehot], axis=0), gains3, ((0,), (0,)))
        rows = (feats[...].astype(jnp.float32) * gains).astype(jnp.bfloat16)
        emb[...] = rows
        for at in range(0, tile, 256):
            c, s = cos_sin(contract(held[...], place[:, at:at + 256], ((1,), (0,))))
            tab[0:kn, at:at + 256] = c
            tab[kn:2 * kn, at:at + 256] = s
        both = jnp.concatenate([rows, cot[...]], axis=1)
        acc[...] += contract(tab[...], both, ((1,), (0,)))

    pltpu.emit_pipeline(
        part,
        grid=(n // tile,),
        in_specs=[
            pl.BlockSpec((3, tile), lambda i: (0, i)),
            pl.BlockSpec((1, tile), lambda i: (0, i)),
            pl.BlockSpec((tile, ch), lambda i: (i, 0)),
            pl.BlockSpec((tile, ch), lambda i: (i, 0)),
        ],
        out_specs=[
            pl.BlockSpec((tile, ch), lambda i: (i, 0)),
            pl.BlockSpec((2 * kn, tile), lambda i: (0, i)),
        ],
    )(frac, species, feats, cot, emb, tab)
    keep[...] = acc[0:kn, :].astype(jnp.bfloat16)
    give[...] = acc[kn:2 * kn, :].astype(jnp.bfloat16)


def factors(core, frac, species, feats, cot, miller, gain, tile=1024):
    n, ch = feats.shape
    kn = miller.shape[1]
    return pl.pallas_call(
        functools.partial(factors_kernel, tile),
        in_specs=[SCALAR, FAR, FAR, FAR, FAR, WHOLE, WHOLE],
        out_specs=[FAR, FAR, WHOLE, WHOLE],
        out_shape=[
            jax.ShapeDtypeStruct((n, ch), jnp.bfloat16),
            jax.ShapeDtypeStruct((2 * kn, n), jnp.bfloat16),
            jax.ShapeDtypeStruct((kn, 2 * ch), jnp.bfloat16),
            jax.ShapeDtypeStruct((kn, 2 * ch), jnp.bfloat16),
        ],
        scratch_shapes=[
            pltpu.VMEM((2 * kn, 2 * ch), jnp.float32),
            pltpu.VMEM((kn, DEPTH), jnp.bfloat16),
        ],
        compiler_params=params(58),
        cost_estimate=cost(8 * n * kn * ch, 8 * n * ch + 4 * n * kn),
        name="factors",
    )(core, frac, species, feats, cot, miller, gain)


def pair_kernel(keep, got, out):
    out[...] = (keep[...].astype(jnp.float32) + got[...].astype(jnp.float32)).astype(jnp.bfloat16)


def pair_of(keep, got):
    return pl.pallas_call(
        pair_kernel,
        in_specs=[WHOLE, WHOLE],
        out_specs=WHOLE,
        out_shape=jax.ShapeDtypeStruct(keep.shape, jnp.bfloat16),
        compiler_params=params(4),
        cost_estimate=cost(10**6, 10**4),
        name="pair",
    )(keep, got)


def panel_kernel(where, spread, weights, out):
    groups, rows, width = spread.shape
    total = spread[0].astype(jnp.float32)
    for i in range(1, groups):
        total += spread[i].astype(jnp.float32)
    w = weights[pl.ds(pl.multiple_of(where[0] * rows, rows), rows), :]
    panel = (total * jnp.concatenate([w] * (width // w.shape[1]), axis=1)).astype(jnp.bfloat16)
    for i in range(groups):
        out[i] = panel


def panel_of(where, spread, weights):
    return pl.pallas_call(
        panel_kernel,
        in_specs=[SCALAR, WHOLE, WHOLE],
        out_specs=WHOLE,
        out_shape=jax.ShapeDtypeStruct(spread.shape, jnp.bfloat16),
        compiler_params=params(4),
        cost_estimate=cost(10**6, 10**4),
        name="panel",
    )(where, spread, weights)


def copies_kernel(core, mine, miller, out):
    blocks, _, ch = out.shape
    kn = miller.shape[1]
    steps = steps_of(miller[...], core[0])
    for i in range(blocks):
        out[i, 0:kn, :] = mine[:, :ch]
        out[i, kn:kn + DEPTH, :] = steps


def copies_of(core, mine, miller, width, blocks):
    kn = miller.shape[1]
    return pl.pallas_call(
        copies_kernel,
        in_specs=[SCALAR, WHOLE, WHOLE],
        out_specs=WHOLE,
        out_shape=jax.ShapeDtypeStruct((blocks, kn + DEPTH, width), jnp.bfloat16),
        compiler_params=params(6),
        cost_estimate=cost(10**6, 10**6),
        name="copies",
    )(core, mine, miller)


def forces_kernel(scale, sign, tab, cot, emb, mine, other, columns, out, spread, rows):
    kn = columns.shape[0]
    tile = cot.shape[0]
    wide = spread.shape[2]
    steps = pl.num_programs(0)
    step = pl.program_id(0)
    each = tile // wide

    @pl.when(step == 0)
    def _():
        for d in range(3):
            spread[d] = jnp.broadcast_to(columns[:, d:d + 1], spread.shape[1:])

    factor = sign[0] * scale
    for j in range(each):
        at = j * wide
        both = jnp.concatenate([cot[at:at + wide, :], emb[at:at + wide, :]], axis=1)
        x = contract(mine[...], both, ((1,), (1,)))
        y = contract(other[...], both, ((1,), (1,)))
        c = tab[0:kn, at:at + wide].astype(jnp.float32)
        s = tab[kn:2 * kn, at:at + wide].astype(jnp.float32)
        grads = c * y - s * x
        for d in range(3):
            rows[pl.ds(d * each * steps + step * each + j, 1), :] = (
                jnp.sum(spread[d] * grads, axis=0, keepdims=True) * factor
            )

    @pl.when(step == steps - 1)
    def _():
        high = rows[...].astype(jnp.bfloat16)
        out[0:rows.shape[0], :] = high
        out[rows.shape[0]:, :] = (rows[...] - high.astype(jnp.float32)).astype(jnp.bfloat16)


def forces_of(sign, tab, cot, emb, mine, other, columns, scale, tile=1024):
    n, ch = cot.shape
    kn = columns.shape[0]
    count = 3 * n // ch
    return pl.pallas_call(
        functools.partial(forces_kernel, scale),
        grid=(n // tile,),
        in_specs=[
            SCALAR,
            pl.BlockSpec((2 * kn, tile), lambda i: (0, i)),
            pl.BlockSpec((tile, ch), lambda i: (i, 0)),
            pl.BlockSpec((tile, ch), lambda i: (i, 0)),
            pl.BlockSpec(mine.shape, lambda i: (0, 0)),
            pl.BlockSpec(other.shape, lambda i: (0, 0)),
            pl.BlockSpec(columns.shape, lambda i: (0, 0)),
        ],
        out_specs=pl.BlockSpec((2 * count, ch), lambda i: (0, 0)),
        out_shape=jax.ShapeDtypeStruct((2 * count, ch), jnp.bfloat16),
        scratch_shapes=[pltpu.VMEM((3, kn, ch), jnp.float32), pltpu.VMEM((count, ch), jnp.float32)],
        compiler_params=params(58),
        cost_estimate=cost(2000 * n * kn, 4 * n * kn + 4 * n * ch),
        name="forces",
    )(sign, tab, cot, emb, mine, other, columns)


def total_kernel(start, parts, out):
    count = (parts.shape[1] - start) // 2
    each = count // out.shape[0]
    wide = parts.shape[2]
    total = jnp.zeros((count, wide), jnp.float32)
    for b in range(parts.shape[0]):
        total += parts[b, start:start + count, :].astype(jnp.float32)
        total += parts[b, start + count:start + 2 * count, :].astype(jnp.float32)
    for d in range(out.shape[0]):
        for j in range(each):
            out[d:d + 1, j * wide:(j + 1) * wide] = total[d * each + j:d * each + j + 1, :]


def total_of(parts, start, n):
    return pl.pallas_call(
        functools.partial(total_kernel, start),
        in_specs=[WHOLE],
        out_specs=WHOLE,
        out_shape=jax.ShapeDtypeStruct((3, n), jnp.float32),
        compiler_params=params(8),
        cost_estimate=cost(10**6, 10**6),
        name="total",
    )(parts)


def rows_of(scale, frac, feats, mine, other):
    blocks = mine.shape[0]
    kn = mine.shape[1] - DEPTH
    place = places(frac[...]).T
    total = jnp.zeros(feats.shape, jnp.float32)
    for b in range(blocks):
        c, s = cos_sin(contract(place, mine[b, kn:kn + DEPTH, :], ((1,), (0,))))
        total += contract(c, mine[b, 0:kn, :], ((1,), (0,)))
        total += contract(s, other[b, 0:kn, :], ((1,), (0,)))
    return (feats[...].astype(jnp.float32) + total * scale).astype(jnp.bfloat16)


def share_kernel(scale, where, force, frac, feats, mine, other, out):
    rows = rows_of(scale, frac, feats, mine, other)
    share = rows.shape[0]
    for b in range(out.shape[0]):
        out[b, 0:share, :] = rows
        out[b, share:, :] = force[...]


def rest_kernel(scale, frac, feats, mine, other, out):
    out[...] = rows_of(scale, frac, feats, mine, other)


def share_of(where, force, frac, feats, mine, other, scale, share):
    n, ch = feats.shape
    blocks = mine.shape[0]
    long = share + force.shape[0]
    return pl.pallas_call(
        functools.partial(share_kernel, scale),
        grid_spec=pltpu.PrefetchScalarGridSpec(
            num_scalar_prefetch=1,
            grid=(1,),
            in_specs=[
                pl.BlockSpec(force.shape, lambda i, at: (0, 0)),
                pl.BlockSpec((3, share), lambda i, at: (0, at[0])),
                pl.BlockSpec((share, ch), lambda i, at: (at[0], 0)),
                pl.BlockSpec(mine.shape, lambda i, at: (0, 0, 0)),
                pl.BlockSpec(other.shape, lambda i, at: (0, 0, 0)),
            ],
            out_specs=pl.BlockSpec((blocks, long, ch), lambda i, at: (0, 0, 0)),
        ),
        out_shape=jax.ShapeDtypeStruct((blocks, long, ch), jnp.bfloat16),
        compiler_params=params(58),
        cost_estimate=cost(10**9, 10**6),
        name="share",
    )(where, force, frac, feats, mine, other)


def rest_of(frac, feats, mine, other, scale, start, tile):
    n, ch = feats.shape
    first = start // tile
    return pl.pallas_call(
        functools.partial(rest_kernel, scale),
        grid=((n - start) // tile,),
        in_specs=[
            pl.BlockSpec((3, tile), lambda i: (0, first + i)),
            pl.BlockSpec((tile, ch), lambda i: (first + i, 0)),
            pl.BlockSpec(mine.shape, lambda i: (0, 0, 0)),
            pl.BlockSpec(other.shape, lambda i: (0, 0, 0)),
        ],
        out_specs=pl.BlockSpec((tile, ch), lambda i: (first + i, 0)),
        out_shape=jax.ShapeDtypeStruct((n, ch), jnp.bfloat16),
        compiler_params=params(58),
        cost_estimate=cost(10**10, 10**6),
        name="rest",
    )(frac, feats, mine, other)


def across(x, axes):
    return lax.all_to_all(x, axes, 0, 0)


def body(frac, species, feats, cot, miller, gain, filter_weight):
    n, ch = feats.shape
    kn = miller.shape[1]
    inv_n = 1.0 / math.sqrt(n * lax.axis_size(("xh", "z", "core")))
    inv_k = 1.0 / math.sqrt(kn * lax.axis_size(ACROSS))
    groups = lax.axis_size(OVER)
    blocks = lax.axis_size(ACROSS)
    rows = kn // groups
    core = jnp.full((1,), lax.axis_index("core").astype(jnp.float32))
    over = jnp.full((1,), lax.axis_index(OVER), jnp.int32)
    spot = jnp.full((1,), lax.axis_index(ACROSS), jnp.int32)

    emb, tab, keep, give = factors(core, frac, species.reshape(1, n), feats, cot, miller, gain)
    pair = pair_of(keep, lax.ppermute(give, "core", SWAP))
    pair, miller = lax.optimization_barrier((pair, miller))
    spread = across(pair.reshape(groups, rows, 2 * ch), OVER)
    weights, columns = prepare(miller, filter_weight, inv_n)
    spread, weights = lax.optimization_barrier((spread, weights))
    mine = across(panel_of(over, spread, weights), OVER).reshape(kn, 2 * ch)

    far = across(copies_of(core, mine, miller, ch, blocks), ACROSS)
    other = lax.ppermute(mine, "core", SWAP)
    force = forces_of(1.0 - 2.0 * core, tab, cot, emb, mine, other, columns, -TWO_PI / BOX * inv_k)
    far, force = lax.optimization_barrier((far, force))
    swapped = lax.ppermute(far, "core", SWAP)
    share = n // blocks * SHARED // 8
    part = share_of(spot, force, frac, feats, far, swapped, inv_k, share)
    part, frac = lax.optimization_barrier((part, frac))
    gathered = across(part, ACROSS)
    rest = rest_of(frac, feats, far, swapped, inv_k, share * blocks, TILE)
    gathered, rest = lax.optimization_barrier((gathered, rest))
    updated = lax.dynamic_update_slice(rest, gathered[:, :share].reshape(share * blocks, ch), (0, 0))
    return updated, total_of(gathered, share, n)


def solution(mesh):
    sizes = dict(mesh.shape)
    fine = Mesh(mesh.devices.reshape(2, sizes["dom"] // 4, 2, 2, sizes["ka"] // 2), ("xh", "z", "core", "xl", "y"))
    dom = ("xh", "z", "core")
    placed = (P(None, dom), P(dom), P(dom, None), P(dom, None), P(None, ACROSS), P(), P())
    return jax.shard_map(
        body,
        mesh=fine,
        in_specs=placed,
        out_specs=(P(dom, None), P(None, dom)),
        check_vma=False,
    )
```

```python
import functools
import math

import jax
import jax.numpy as jnp
from jax import lax
from jax.experimental import pallas as pl
from jax.experimental.pallas import tpu as pltpu
from jax.sharding import Mesh, PartitionSpec as P

TWO_PI = 6.283185307179586
BOX = 64.0
MIB = 1024 * 1024
SINE = (4.4428679, -7.30744342, 3.59478803, -0.7843739)
OVER = ("xh", "z")
ACROSS = ("xl", "y")
SWAP = [(0, 1), (1, 0)]
DEPTH = 16
SHARED = 4
TILE = 1024
WHOLE = pl.BlockSpec(memory_space=pltpu.VMEM)
SCALAR = pl.BlockSpec(memory_space=pltpu.SMEM)
FAR = pl.BlockSpec(memory_space=pltpu.HBM)


def triple(x):
    hi = x.astype(jnp.bfloat16)
    rest = x - hi.astype(jnp.float32)
    mid = rest.astype(jnp.bfloat16)
    low = (rest - mid.astype(jnp.float32)).astype(jnp.bfloat16)
    return [hi, mid, low]


def places(frac):
    n = frac.shape[1]
    rest = DEPTH - 10
    return jnp.concatenate(
        triple(frac) + [jnp.ones((1, n), jnp.bfloat16), jnp.zeros((rest, n), jnp.bfloat16)], axis=0
    )


def contract(left, right, dims):
    return lax.dot_general(left, right, (dims, ((), ())), preferred_element_type=jnp.float32)


def cos_sin(turns):
    r = turns - jnp.round(turns)
    t = r * r
    s = (((SINE[3] * t + SINE[2]) * t + SINE[1]) * t + SINE[0]) * r
    square = s * s
    rest = 2.000004 - square
    return (1.0 - square).astype(jnp.bfloat16), (s * (rest * lax.rsqrt(rest))).astype(jnp.bfloat16)


def params(mib):
    return pltpu.CompilerParams(vmem_limit_bytes=mib * MIB)


def cost(flops, moved):
    return pl.CostEstimate(flops=flops, bytes_accessed=moved, transcendentals=0)


def steps_of(miller, core):
    kn = miller.shape[1]
    mills = miller.astype(jnp.float32) * (1.0 - 2.0 * core)
    rows = [mills, mills, mills, jnp.full((1, kn), 0.25 * core), jnp.zeros((DEPTH - 10, kn), jnp.float32)]
    return jnp.concatenate(rows, axis=0).astype(jnp.bfloat16)


def prepare_kernel(scale, miller, filter_weight, weights, columns):
    kn = miller.shape[1]
    column = jnp.concatenate([miller[...].astype(jnp.float32), jnp.zeros((5, kn), jnp.float32)], axis=0).T
    columns[...] = column
    length = jnp.sqrt(jnp.sum(column * column, axis=1, keepdims=True))
    count = filter_weight.shape[0]
    centres = lax.broadcasted_iota(jnp.int32, (1, count), 1).astype(jnp.float32) * (14.0 / (count - 1))
    basis = jnp.exp(-((length - centres) ** 2))
    weights[...] = scale * jnp.dot(
        basis, filter_weight[...], precision=lax.Precision.HIGHEST, preferred_element_type=jnp.float32
    )


def prepare(miller, filter_weight, scale):
    kn = miller.shape[1]
    return pl.pallas_call(
        functools.partial(prepare_kernel, scale),
        in_specs=[WHOLE, WHOLE],
        out_specs=[WHOLE] * 2,
        out_shape=[
            jax.ShapeDtypeStruct((kn, filter_weight.shape[1]), jnp.float32),
            jax.ShapeDtypeStruct((kn, 8), jnp.float32),
        ],
        compiler_params=params(4),
        cost_estimate=cost(10**6, 10**5),
        name="prepare",
    )(miller, filter_weight)


def embed(feats, species, gains3):
    kinds = gains3.shape[0] // 3
    onehot = (lax.broadcasted_iota(jnp.int32, (kinds, species.shape[1]), 0) == species).astype(jnp.float32)
    onehot = onehot.astype(jnp.bfloat16)
    gains = contract(jnp.concatenate([onehot, onehot, onehot], axis=0), gains3, ((0,), (0,)))
    return (feats.astype(jnp.float32) * gains).astype(jnp.bfloat16)


def factors_kernel(core, frac, species, feats, cot, miller, gain, keep, give, acc, held, tab):
    step = pl.program_id(0)
    kn = miller.shape[1]
    tile = frac.shape[1]

    @pl.when(step == 0)
    def _():
        acc[...] = jnp.zeros_like(acc)
        held[...] = steps_of(miller[...], core[0]).T

    place = places(frac[...])
    rows = embed(feats[...], species[...], jnp.concatenate(triple(gain[...]), axis=0))
    for at in range(0, tile, 256):
        c, s = cos_sin(contract(held[...], place[:, at:at + 256], ((1,), (0,))))
        tab[0:kn, at:at + 256] = c
        tab[kn:2 * kn, at:at + 256] = s
    both = jnp.concatenate([rows, cot[...]], axis=1)
    acc[...] += contract(tab[...], both, ((1,), (0,)))

    @pl.when(step == pl.num_programs(0) - 1)
    def _():
        keep[...] = acc[0:kn, :].astype(jnp.bfloat16)
        give[...] = acc[kn:2 * kn, :].astype(jnp.bfloat16)


def factors(core, frac, species, feats, cot, miller, gain, tile=1024):
    n, ch = feats.shape
    kn = miller.shape[1]
    return pl.pallas_call(
        factors_kernel,
        grid=(n // tile,),
        in_specs=[
            SCALAR,
            pl.BlockSpec((3, tile), lambda i: (0, i)),
            pl.BlockSpec((1, tile), lambda i: (0, i)),
            pl.BlockSpec((tile, ch), lambda i: (i, 0)),
            pl.BlockSpec((tile, ch), lambda i: (i, 0)),
            pl.BlockSpec(miller.shape, lambda i: (0, 0)),
            pl.BlockSpec(gain.shape, lambda i: (0, 0)),
        ],
        out_specs=[pl.BlockSpec((kn, 2 * ch), lambda i: (0, 0))] * 2,
        out_shape=[jax.ShapeDtypeStruct((kn, 2 * ch), jnp.bfloat16)] * 2,
        scratch_shapes=[
            pltpu.VMEM((2 * kn, 2 * ch), jnp.float32),
            pltpu.VMEM((kn, DEPTH), jnp.bfloat16),
            pltpu.VMEM((2 * kn, tile), jnp.bfloat16),
        ],
        compiler_params=params(58),
        cost_estimate=cost(8 * n * kn * ch, 8 * n * ch + 4 * n * kn),
        name="factors",
    )(core, frac, species, feats, cot, miller, gain)


def pair_kernel(keep, got, out):
    out[...] = (keep[...].astype(jnp.float32) + got[...].astype(jnp.float32)).astype(jnp.bfloat16)


def pair_of(keep, got):
    return pl.pallas_call(
        pair_kernel,
        in_specs=[WHOLE, WHOLE],
        out_specs=WHOLE,
        out_shape=jax.ShapeDtypeStruct(keep.shape, jnp.bfloat16),
        compiler_params=params(4),
        cost_estimate=cost(10**6, 10**4),
        name="pair",
    )(keep, got)


def panel_kernel(where, spread, weights, out):
    groups, rows, width = spread.shape
    total = spread[0].astype(jnp.float32)
    for i in range(1, groups):
        total += spread[i].astype(jnp.float32)
    w = weights[pl.ds(pl.multiple_of(where[0] * rows, rows), rows), :]
    panel = (total * jnp.concatenate([w] * (width // w.shape[1]), axis=1)).astype(jnp.bfloat16)
    for i in range(groups):
        out[i] = panel


def panel_of(where, spread, weights):
    return pl.pallas_call(
        panel_kernel,
        in_specs=[SCALAR, WHOLE, WHOLE],
        out_specs=WHOLE,
        out_shape=jax.ShapeDtypeStruct(spread.shape, jnp.bfloat16),
        compiler_params=params(4),
        cost_estimate=cost(10**6, 10**4),
        name="panel",
    )(where, spread, weights)


def copies_kernel(core, mine, miller, out):
    blocks, _, ch = out.shape
    kn = miller.shape[1]
    steps = steps_of(miller[...], core[0])
    for i in range(blocks):
        out[i, 0:kn, :] = mine[:, :ch]
        out[i, kn:kn + DEPTH, :] = steps


def copies_of(core, mine, miller, width, blocks):
    kn = miller.shape[1]
    return pl.pallas_call(
        copies_kernel,
        in_specs=[SCALAR, WHOLE, WHOLE],
        out_specs=WHOLE,
        out_shape=jax.ShapeDtypeStruct((blocks, kn + DEPTH, width), jnp.bfloat16),
        compiler_params=params(6),
        cost_estimate=cost(10**6, 10**6),
        name="copies",
    )(core, mine, miller)


def forces_kernel(scale, core, frac, species, feats, cot, miller, gain, mine, other, columns, out, held, spread, rows):
    kn = columns.shape[0]
    tile = cot.shape[0]
    wide = spread.shape[2]
    steps = pl.num_programs(0)
    step = pl.program_id(0)
    each = tile // wide

    @pl.when(step == 0)
    def _():
        held[...] = steps_of(miller[...], core[0]).T
        for d in range(3):
            spread[d] = jnp.broadcast_to(columns[:, d:d + 1], spread.shape[1:])

    factor = (1.0 - 2.0 * core[0]) * scale
    place = places(frac[...])
    emb = embed(feats[...], species[...], jnp.concatenate(triple(gain[...]), axis=0))
    for j in range(each):
        at = j * wide
        both = jnp.concatenate([cot[at:at + wide, :], emb[at:at + wide, :]], axis=1)
        x = contract(mine[...], both, ((1,), (1,)))
        y = contract(other[...], both, ((1,), (1,)))
        c, s = cos_sin(contract(held[...], place[:, at:at + wide], ((1,), (0,))))
        grads = c.astype(jnp.float32) * y - s.astype(jnp.float32) * x
        for d in range(3):
            rows[pl.ds(d * each * steps + step * each + j, 1), :] = (
                jnp.sum(spread[d] * grads, axis=0, keepdims=True) * factor
            )

    @pl.when(step == steps - 1)
    def _():
        out[...] = rows[...].astype(jnp.bfloat16)


def forces_of(core, frac, species, feats, cot, miller, gain, mine, other, columns, scale, tile=1024):
    n, ch = cot.shape
    kn = columns.shape[0]
    count = 3 * n // ch
    return pl.pallas_call(
        functools.partial(forces_kernel, scale),
        grid=(n // tile,),
        in_specs=[
            SCALAR,
            pl.BlockSpec((3, tile), lambda i: (0, i)),
            pl.BlockSpec((1, tile), lambda i: (0, i)),
            pl.BlockSpec((tile, ch), lambda i: (i, 0)),
            pl.BlockSpec((tile, ch), lambda i: (i, 0)),
            pl.BlockSpec(miller.shape, lambda i: (0, 0)),
            pl.BlockSpec(gain.shape, lambda i: (0, 0)),
            pl.BlockSpec(mine.shape, lambda i: (0, 0)),
            pl.BlockSpec(other.shape, lambda i: (0, 0)),
            pl.BlockSpec(columns.shape, lambda i: (0, 0)),
        ],
        out_specs=pl.BlockSpec((count, ch), lambda i: (0, 0)),
        out_shape=jax.ShapeDtypeStruct((count, ch), jnp.bfloat16),
        scratch_shapes=[
            pltpu.VMEM((kn, DEPTH), jnp.bfloat16),
            pltpu.VMEM((3, kn, ch), jnp.float32),
            pltpu.VMEM((count, ch), jnp.float32),
        ],
        compiler_params=params(58),
        cost_estimate=cost(2000 * n * kn, 4 * n * kn + 4 * n * ch),
        name="forces",
    )(core, frac, species, feats, cot, miller, gain, mine, other, columns)


def finish_kernel(share, parts, rest, out, forces, sems):
    blocks, long, wide = parts.shape
    copies = [
        pltpu.make_async_copy(parts.at[b, pl.ds(0, share), :], out.at[pl.ds(b * share, share), :], sems.at[b])
        for b in range(blocks)
    ]
    for copy in copies:
        copy.start()
    count = long - share
    each = count // forces.shape[0]
    total = jnp.zeros((count, wide), jnp.float32)
    for b in range(blocks):
        total += parts[b, share:share + count, :].astype(jnp.float32)
    for d in range(forces.shape[0]):
        for j in range(each):
            forces[d:d + 1, j * wide:(j + 1) * wide] = total[d * each + j:d * each + j + 1, :]
    for copy in copies:
        copy.wait()


def finish(parts, rest, share):
    n, ch = rest.shape
    return pl.pallas_call(
        functools.partial(finish_kernel, share),
        in_specs=[WHOLE, FAR],
        out_specs=[FAR, WHOLE],
        out_shape=[jax.ShapeDtypeStruct((n, ch), jnp.bfloat16), jax.ShapeDtypeStruct((3, n), jnp.float32)],
        scratch_shapes=[pltpu.SemaphoreType.DMA((parts.shape[0],))],
        input_output_aliases={1: 0},
        compiler_params=params(8),
        cost_estimate=cost(10**6, 10**6),
        name="finish",
    )(parts, rest)


def half_kernel(frac, mine, total, table):
    kn = mine.shape[1] - DEPTH
    place = places(frac[...]).T
    sums = jnp.zeros(total.shape, jnp.float32)
    for b in range(mine.shape[0]):
        c, s = cos_sin(contract(place, mine[b, kn:kn + DEPTH, :], ((1,), (0,))))
        sums += contract(c, mine[b, 0:kn, :], ((1,), (0,)))
        table[:, b * kn:(b + 1) * kn] = s
    total[...] = sums


def half_of(frac, mine):
    n = frac.shape[1]
    blocks, long, ch = mine.shape
    return pl.pallas_call(
        half_kernel,
        in_specs=[WHOLE, WHOLE],
        out_specs=[WHOLE, WHOLE],
        out_shape=[
            jax.ShapeDtypeStruct((n, ch), jnp.float32),
            jax.ShapeDtypeStruct((n, blocks * (long - DEPTH)), jnp.bfloat16),
        ],
        compiler_params=params(8),
        cost_estimate=cost(2 * 10**9, 10**6),
        name="half",
    )(frac, mine)


def share_kernel(scale, total, table, other, feats, force, out):
    kn = other.shape[1] - DEPTH
    share = feats.shape[0]
    sums = total[...]
    for b in range(other.shape[0]):
        sums += contract(table[:, b * kn:(b + 1) * kn], other[b, 0:kn, :], ((1,), (0,)))
    rows = (feats[...].astype(jnp.float32) + sums * scale).astype(jnp.bfloat16)
    for b in range(out.shape[0]):
        out[b, 0:share, :] = rows
        out[b, share:, :] = force[...]


def share_of(total, table, other, feats, force, scale):
    share, ch = feats.shape
    return pl.pallas_call(
        functools.partial(share_kernel, scale),
        in_specs=[WHOLE] * 5,
        out_specs=WHOLE,
        out_shape=jax.ShapeDtypeStruct((other.shape[0], share + force.shape[0], ch), jnp.bfloat16),
        compiler_params=params(8),
        cost_estimate=cost(10**9, 10**6),
        name="share",
    )(total, table, other, feats, force)


def rest_kernel(scale, frac, feats, mine, other, out):
    blocks = mine.shape[0]
    kn = mine.shape[1] - DEPTH
    place = places(frac[...]).T
    for at in range(0, feats.shape[0], 256):
        here = slice(at, at + 256)
        total = jnp.zeros((256, feats.shape[1]), jnp.float32)
        for b in range(blocks):
            c, s = cos_sin(contract(place[here], mine[b, kn:kn + DEPTH, :], ((1,), (0,))))
            total += contract(c, mine[b, 0:kn, :], ((1,), (0,)))
            total += contract(s, other[b, 0:kn, :], ((1,), (0,)))
        out[here, :] = (feats[here, :].astype(jnp.float32) + total * scale).astype(jnp.bfloat16)


def rest_of(frac, feats, mine, other, scale, start, tile):
    n, ch = feats.shape
    first = start // tile
    return pl.pallas_call(
        functools.partial(rest_kernel, scale),
        grid=((n - start) // tile,),
        in_specs=[
            pl.BlockSpec((3, tile), lambda i: (0, first + i)),
            pl.BlockSpec((tile, ch), lambda i: (first + i, 0)),
            pl.BlockSpec(mine.shape, lambda i: (0, 0, 0)),
            pl.BlockSpec(other.shape, lambda i: (0, 0, 0)),
        ],
        out_specs=pl.BlockSpec((tile, ch), lambda i: (first + i, 0)),
        out_shape=jax.ShapeDtypeStruct((n, ch), jnp.bfloat16),
        compiler_params=params(58),
        cost_estimate=cost(10**10, 10**6),
        name="rest",
    )(frac, feats, mine, other)


def across(x, axes):
    return lax.all_to_all(x, axes, 0, 0)


def body(frac, species, feats, cot, miller, gain, filter_weight):
    n, ch = feats.shape
    kn = miller.shape[1]
    inv_n = 1.0 / math.sqrt(n * lax.axis_size(("xh", "z", "core")))
    inv_k = 1.0 / math.sqrt(kn * lax.axis_size(ACROSS))
    groups = lax.axis_size(OVER)
    blocks = lax.axis_size(ACROSS)
    rows = kn // groups
    core = jnp.full((1,), lax.axis_index("core").astype(jnp.float32))
    over = jnp.full((1,), lax.axis_index(OVER), jnp.int32)
    spot = jnp.full((1,), lax.axis_index(ACROSS), jnp.int32)

    kinds = species.reshape(1, n)
    keep, give = factors(core, frac, kinds, feats, cot, miller, gain)
    pair = pair_of(keep, lax.ppermute(give, "core", SWAP))
    share = n // blocks * SHARED // 8
    pair, miller, some_frac, some_feats = lax.optimization_barrier((pair, miller, frac, feats))
    spread = across(pair.reshape(groups, rows, 2 * ch), OVER)
    weights, columns = prepare(miller, filter_weight, inv_n)
    some_frac = lax.dynamic_slice_in_dim(some_frac, spot[0] * share, share, axis=1)
    some_feats = lax.dynamic_slice_in_dim(some_feats, spot[0] * share, share, axis=0)
    spread, weights, some_frac, some_feats = lax.optimization_barrier((spread, weights, some_frac, some_feats))
    mine = across(panel_of(over, spread, weights), OVER).reshape(kn, 2 * ch)

    far = across(copies_of(core, mine, miller, ch, blocks), ACROSS)
    other = lax.ppermute(mine, "core", SWAP)
    scale = -TWO_PI / BOX * inv_k
    force = forces_of(core, frac, kinds, feats, cot, miller, gain, mine, other, columns, scale)
    far, force = lax.optimization_barrier((far, force))
    swapped = lax.ppermute(far, "core", SWAP)
    total, table = half_of(some_frac, far)
    part = share_of(total, table, swapped, some_feats, force, inv_k)
    part, frac = lax.optimization_barrier((part, frac))
    gathered = across(part, ACROSS)
    rest = rest_of(frac, feats, far, swapped, inv_k, share * blocks, TILE)
    gathered, rest = lax.optimization_barrier((gathered, rest))
    return tuple(finish(gathered, rest, share))


def solution(mesh):
    sizes = dict(mesh.shape)
    fine = Mesh(mesh.devices.reshape(2, sizes["dom"] // 4, 2, 2, sizes["ka"] // 2), ("xh", "z", "core", "xl", "y"))
    dom = ("xh", "z", "core")
    placed = (P(None, dom), P(dom), P(dom, None), P(dom, None), P(None, ACROSS), P(), P())
    return jax.shard_map(
        body,
        mesh=fine,
        in_specs=placed,
        out_specs=(P(dom, None), P(None, dom)),
        check_vma=False,
    )
```

```python
import functools
import math

import jax
import jax.numpy as jnp
from jax import lax
from jax.experimental import pallas as pl
from jax.experimental.pallas import tpu as pltpu
from jax.sharding import Mesh, PartitionSpec as P

TWO_PI = 6.283185307179586
BOX = 64.0
MIB = 1024 * 1024
SINE = (4.4428679, -7.30744342, 3.59478803, -0.7843739)
OVER = ("xh", "z")
ACROSS = ("xl", "y")
SWAP = [(0, 1), (1, 0)]
DEPTH = 16
SHARED = 4
TILE = 1024
WHOLE = pl.BlockSpec(memory_space=pltpu.VMEM)
SCALAR = pl.BlockSpec(memory_space=pltpu.SMEM)
FAR = pl.BlockSpec(memory_space=pltpu.HBM)


def triple(x):
    hi = x.astype(jnp.bfloat16)
    rest = x - hi.astype(jnp.float32)
    mid = rest.astype(jnp.bfloat16)
    low = (rest - mid.astype(jnp.float32)).astype(jnp.bfloat16)
    return [hi, mid, low]


def places(frac):
    n = frac.shape[1]
    rest = DEPTH - 10
    return jnp.concatenate(
        triple(frac) + [jnp.ones((1, n), jnp.bfloat16), jnp.zeros((rest, n), jnp.bfloat16)], axis=0
    )


def contract(left, right, dims):
    return lax.dot_general(left, right, (dims, ((), ())), preferred_element_type=jnp.float32)


def cos_sin(turns):
    r = turns - jnp.round(turns)
    t = r * r
    s = (((SINE[3] * t + SINE[2]) * t + SINE[1]) * t + SINE[0]) * r
    square = s * s
    rest = 2.000004 - square
    return (1.0 - square).astype(jnp.bfloat16), (s * (rest * lax.rsqrt(rest))).astype(jnp.bfloat16)


def params(mib):
    return pltpu.CompilerParams(vmem_limit_bytes=mib * MIB)


def cost(flops, moved):
    return pl.CostEstimate(flops=flops, bytes_accessed=moved, transcendentals=0)


def steps_of(miller, core):
    kn = miller.shape[1]
    mills = miller.astype(jnp.float32) * (1.0 - 2.0 * core)
    rows = [mills, mills, mills, jnp.full((1, kn), 0.25 * core), jnp.zeros((DEPTH - 10, kn), jnp.float32)]
    return jnp.concatenate(rows, axis=0).astype(jnp.bfloat16)


def prepare_kernel(scale, miller, filter_weight, weights, columns):
    kn = miller.shape[1]
    column = jnp.concatenate([miller[...].astype(jnp.float32), jnp.zeros((5, kn), jnp.float32)], axis=0).T
    columns[...] = column
    length = jnp.sqrt(jnp.sum(column * column, axis=1, keepdims=True))
    count = filter_weight.shape[0]
    centres = lax.broadcasted_iota(jnp.int32, (1, count), 1).astype(jnp.float32) * (14.0 / (count - 1))
    basis = jnp.exp(-((length - centres) ** 2))
    weights[...] = scale * jnp.dot(
        basis, filter_weight[...], precision=lax.Precision.HIGHEST, preferred_element_type=jnp.float32
    )


def prepare(miller, filter_weight, scale):
    kn = miller.shape[1]
    return pl.pallas_call(
        functools.partial(prepare_kernel, scale),
        in_specs=[WHOLE, WHOLE],
        out_specs=[WHOLE] * 2,
        out_shape=[
            jax.ShapeDtypeStruct((kn, filter_weight.shape[1]), jnp.float32),
            jax.ShapeDtypeStruct((kn, 8), jnp.float32),
        ],
        compiler_params=params(4),
        cost_estimate=cost(10**6, 10**5),
        name="prepare",
    )(miller, filter_weight)


def embed(feats, species, gains3):
    kinds = gains3.shape[0] // 3
    onehot = (lax.broadcasted_iota(jnp.int32, (kinds, species.shape[1]), 0) == species).astype(jnp.float32)
    onehot = onehot.astype(jnp.bfloat16)
    gains = contract(jnp.concatenate([onehot, onehot, onehot], axis=0), gains3, ((0,), (0,)))
    return (feats.astype(jnp.float32) * gains).astype(jnp.bfloat16)


def factors_kernel(core, frac, species, feats, cot, miller, gain, keep, give, acc, held, tab):
    step = pl.program_id(0)
    kn = miller.shape[1]
    tile = frac.shape[1]

    @pl.when(step == 0)
    def _():
        acc[...] = jnp.zeros_like(acc)
        held[...] = steps_of(miller[...], core[0]).T

    place = places(frac[...])
    rows = embed(feats[...], species[...], jnp.concatenate(triple(gain[...]), axis=0))
    for at in range(0, tile, 256):
        c, s = cos_sin(contract(held[...], place[:, at:at + 256], ((1,), (0,))))
        tab[0:kn, at:at + 256] = c
        tab[kn:2 * kn, at:at + 256] = s
    both = jnp.concatenate([rows, cot[...]], axis=1)
    acc[...] += contract(tab[...], both, ((1,), (0,)))

    @pl.when(step == pl.num_programs(0) - 1)
    def _():
        keep[...] = acc[0:kn, :].astype(jnp.bfloat16)
        give[...] = acc[kn:2 * kn, :].astype(jnp.bfloat16)


def factors(core, frac, species, feats, cot, miller, gain, tile=2048):
    n, ch = feats.shape
    kn = miller.shape[1]
    return pl.pallas_call(
        factors_kernel,
        grid=(n // tile,),
        in_specs=[
            SCALAR,
            pl.BlockSpec((3, tile), lambda i: (0, i)),
            pl.BlockSpec((1, tile), lambda i: (0, i)),
            pl.BlockSpec((tile, ch), lambda i: (i, 0)),
            pl.BlockSpec((tile, ch), lambda i: (i, 0)),
            pl.BlockSpec(miller.shape, lambda i: (0, 0)),
            pl.BlockSpec(gain.shape, lambda i: (0, 0)),
        ],
        out_specs=[pl.BlockSpec((kn, 2 * ch), lambda i: (0, 0))] * 2,
        out_shape=[jax.ShapeDtypeStruct((kn, 2 * ch), jnp.bfloat16)] * 2,
        scratch_shapes=[
            pltpu.VMEM((2 * kn, 2 * ch), jnp.float32),
            pltpu.VMEM((kn, DEPTH), jnp.bfloat16),
            pltpu.VMEM((2 * kn, tile), jnp.bfloat16),
        ],
        compiler_params=params(58),
        cost_estimate=cost(8 * n * kn * ch, 8 * n * ch + 4 * n * kn),
        name="factors",
    )(core, frac, species, feats, cot, miller, gain)


def pair_kernel(keep, got, out):
    out[...] = (keep[...].astype(jnp.float32) + got[...].astype(jnp.float32)).astype(jnp.bfloat16)


def pair_of(keep, got):
    return pl.pallas_call(
        pair_kernel,
        in_specs=[WHOLE, WHOLE],
        out_specs=WHOLE,
        out_shape=jax.ShapeDtypeStruct(keep.shape, jnp.bfloat16),
        compiler_params=params(4),
        cost_estimate=cost(10**6, 10**4),
        name="pair",
    )(keep, got)


def panel_kernel(where, spread, weights, out):
    groups, rows, width = spread.shape
    total = spread[0].astype(jnp.float32)
    for i in range(1, groups):
        total += spread[i].astype(jnp.float32)
    w = weights[pl.ds(pl.multiple_of(where[0] * rows, rows), rows), :]
    panel = (total * jnp.concatenate([w] * (width // w.shape[1]), axis=1)).astype(jnp.bfloat16)
    for i in range(groups):
        out[i] = panel


def panel_of(where, spread, weights):
    return pl.pallas_call(
        panel_kernel,
        in_specs=[SCALAR, WHOLE, WHOLE],
        out_specs=WHOLE,
        out_shape=jax.ShapeDtypeStruct(spread.shape, jnp.bfloat16),
        compiler_params=params(4),
        cost_estimate=cost(10**6, 10**4),
        name="panel",
    )(where, spread, weights)


def copies_kernel(core, mine, miller, out):
    blocks, _, ch = out.shape
    kn = miller.shape[1]
    steps = steps_of(miller[...], core[0])
    for i in range(blocks):
        out[i, 0:kn, :] = mine[:, :ch]
        out[i, kn:kn + DEPTH, :] = steps


def copies_of(core, mine, miller, width, blocks):
    kn = miller.shape[1]
    return pl.pallas_call(
        copies_kernel,
        in_specs=[SCALAR, WHOLE, WHOLE],
        out_specs=WHOLE,
        out_shape=jax.ShapeDtypeStruct((blocks, kn + DEPTH, width), jnp.bfloat16),
        compiler_params=params(6),
        cost_estimate=cost(10**6, 10**6),
        name="copies",
    )(core, mine, miller)


def forces_kernel(scale, core, frac, species, feats, cot, miller, gain, mine, other, columns, out, held, spread, rows):
    kn = columns.shape[0]
    tile = cot.shape[0]
    wide = spread.shape[2]
    steps = pl.num_programs(0)
    step = pl.program_id(0)
    each = tile // wide

    @pl.when(step == 0)
    def _():
        held[...] = steps_of(miller[...], core[0]).T
        for d in range(3):
            spread[d] = jnp.broadcast_to(columns[:, d:d + 1], spread.shape[1:])

    factor = (1.0 - 2.0 * core[0]) * scale
    place = places(frac[...])
    emb = embed(feats[...], species[...], jnp.concatenate(triple(gain[...]), axis=0))
    for j in range(each):
        at = j * wide
        both = jnp.concatenate([cot[at:at + wide, :], emb[at:at + wide, :]], axis=1)
        x = contract(mine[...], both, ((1,), (1,)))
        y = contract(other[...], both, ((1,), (1,)))
        c, s = cos_sin(contract(held[...], place[:, at:at + wide], ((1,), (0,))))
        grads = c.astype(jnp.float32) * y - s.astype(jnp.float32) * x
        for d in range(3):
            rows[pl.ds(d * each * steps + step * each + j, 1), :] = (
                jnp.sum(spread[d] * grads, axis=0, keepdims=True) * factor
            )

    @pl.when(step == steps - 1)
    def _():
        out[...] = rows[...].astype(jnp.bfloat16)


def forces_of(core, frac, species, feats, cot, miller, gain, mine, other, columns, scale, tile=1024):
    n, ch = cot.shape
    kn = columns.shape[0]
    count = 3 * n // ch
    return pl.pallas_call(
        functools.partial(forces_kernel, scale),
        grid=(n // tile,),
        in_specs=[
            SCALAR,
            pl.BlockSpec((3, tile), lambda i: (0, i)),
            pl.BlockSpec((1, tile), lambda i: (0, i)),
            pl.BlockSpec((tile, ch), lambda i: (i, 0)),
            pl.BlockSpec((tile, ch), lambda i: (i, 0)),
            pl.BlockSpec(miller.shape, lambda i: (0, 0)),
            pl.BlockSpec(gain.shape, lambda i: (0, 0)),
            pl.BlockSpec(mine.shape, lambda i: (0, 0)),
            pl.BlockSpec(other.shape, lambda i: (0, 0)),
            pl.BlockSpec(columns.shape, lambda i: (0, 0)),
        ],
        out_specs=pl.BlockSpec((count, ch), lambda i: (0, 0)),
        out_shape=jax.ShapeDtypeStruct((count, ch), jnp.bfloat16),
        scratch_shapes=[
            pltpu.VMEM((kn, DEPTH), jnp.bfloat16),
            pltpu.VMEM((3, kn, ch), jnp.float32),
            pltpu.VMEM((count, ch), jnp.float32),
        ],
        compiler_params=params(58),
        cost_estimate=cost(2000 * n * kn, 4 * n * kn + 4 * n * ch),
        name="forces",
    )(core, frac, species, feats, cot, miller, gain, mine, other, columns)


def finish_kernel(share, parts, rest, out, forces, sems):
    blocks, long, wide = parts.shape
    copies = [
        pltpu.make_async_copy(parts.at[b, pl.ds(0, share), :], out.at[pl.ds(b * share, share), :], sems.at[b])
        for b in range(blocks)
    ]
    for copy in copies:
        copy.start()
    count = long - share
    each = count // forces.shape[0]
    total = jnp.zeros((count, wide), jnp.float32)
    for b in range(blocks):
        total += parts[b, share:share + count, :].astype(jnp.float32)
    for d in range(forces.shape[0]):
        for j in range(each):
            forces[d:d + 1, j * wide:(j + 1) * wide] = total[d * each + j:d * each + j + 1, :]
    for copy in copies:
        copy.wait()


def finish(parts, rest, share):
    n, ch = rest.shape
    return pl.pallas_call(
        functools.partial(finish_kernel, share),
        in_specs=[WHOLE, FAR],
        out_specs=[FAR, WHOLE],
        out_shape=[jax.ShapeDtypeStruct((n, ch), jnp.bfloat16), jax.ShapeDtypeStruct((3, n), jnp.float32)],
        scratch_shapes=[pltpu.SemaphoreType.DMA((parts.shape[0],))],
        input_output_aliases={1: 0},
        compiler_params=params(8),
        cost_estimate=cost(10**6, 10**6),
        name="finish",
    )(parts, rest)


def half_kernel(frac, mine, total, table):
    kn = mine.shape[1] - DEPTH
    place = places(frac[...]).T
    sums = jnp.zeros(total.shape, jnp.float32)
    for b in range(mine.shape[0]):
        c, s = cos_sin(contract(place, mine[b, kn:kn + DEPTH, :], ((1,), (0,))))
        sums += contract(c, mine[b, 0:kn, :], ((1,), (0,)))
        table[:, b * kn:(b + 1) * kn] = s
    total[...] = sums


def half_of(frac, mine):
    n = frac.shape[1]
    blocks, long, ch = mine.shape
    return pl.pallas_call(
        half_kernel,
        in_specs=[WHOLE, WHOLE],
        out_specs=[WHOLE, WHOLE],
        out_shape=[
            jax.ShapeDtypeStruct((n, ch), jnp.float32),
            jax.ShapeDtypeStruct((n, blocks * (long - DEPTH)), jnp.bfloat16),
        ],
        compiler_params=params(8),
        cost_estimate=cost(2 * 10**9, 10**6),
        name="half",
    )(frac, mine)


def share_kernel(scale, total, table, other, feats, force, out):
    kn = other.shape[1] - DEPTH
    share = feats.shape[0]
    sums = total[...]
    for b in range(other.shape[0]):
        sums += contract(table[:, b * kn:(b + 1) * kn], other[b, 0:kn, :], ((1,), (0,)))
    rows = (feats[...].astype(jnp.float32) + sums * scale).astype(jnp.bfloat16)
    for b in range(out.shape[0]):
        out[b, 0:share, :] = rows
        out[b, share:, :] = force[...]


def share_of(total, table, other, feats, force, scale):
    share, ch = feats.shape
    return pl.pallas_call(
        functools.partial(share_kernel, scale),
        in_specs=[WHOLE] * 5,
        out_specs=WHOLE,
        out_shape=jax.ShapeDtypeStruct((other.shape[0], share + force.shape[0], ch), jnp.bfloat16),
        compiler_params=params(8),
        cost_estimate=cost(10**9, 10**6),
        name="share",
    )(total, table, other, feats, force)


def rest_kernel(scale, frac, feats, mine, other, out):
    blocks = mine.shape[0]
    kn = mine.shape[1] - DEPTH
    rows = 256
    place = places(frac[...]).T
    panels = [jnp.concatenate([p[b, 0:kn, :] for b in range(blocks)], axis=0) for p in (mine, other)]

    def tables_at(at):
        pairs = [
            cos_sin(contract(place[at:at + rows], mine[b, kn:kn + DEPTH, :], ((1,), (0,)))) for b in range(blocks)
        ]
        return [jnp.concatenate(table, axis=1) for table in zip(*pairs)]

    after = tables_at(0)
    for at in range(0, feats.shape[0], rows):
        here = slice(at, at + rows)
        first, second = after
        if at + rows < feats.shape[0]:
            after = tables_at(at + rows)
        total = contract(first, panels[0], ((1,), (0,))) + contract(second, panels[1], ((1,), (0,)))
        out[here, :] = (feats[here, :].astype(jnp.float32) + total * scale).astype(jnp.bfloat16)


def rest_of(frac, feats, mine, other, scale, start, tile):
    n, ch = feats.shape
    first = start // tile
    return pl.pallas_call(
        functools.partial(rest_kernel, scale),
        grid=((n - start) // tile,),
        in_specs=[
            pl.BlockSpec((3, tile), lambda i: (0, first + i)),
            pl.BlockSpec((tile, ch), lambda i: (first + i, 0)),
            pl.BlockSpec(mine.shape, lambda i: (0, 0, 0)),
            pl.BlockSpec(other.shape, lambda i: (0, 0, 0)),
        ],
        out_specs=pl.BlockSpec((tile, ch), lambda i: (first + i, 0)),
        out_shape=jax.ShapeDtypeStruct((n, ch), jnp.bfloat16),
        compiler_params=params(58),
        cost_estimate=cost(10**10, 10**6),
        name="rest",
    )(frac, feats, mine, other)


def across(x, axes):
    return lax.all_to_all(x, axes, 0, 0)


def body(frac, species, feats, cot, miller, gain, filter_weight):
    n, ch = feats.shape
    kn = miller.shape[1]
    inv_n = 1.0 / math.sqrt(n * lax.axis_size(("xh", "z", "core")))
    inv_k = 1.0 / math.sqrt(kn * lax.axis_size(ACROSS))
    groups = lax.axis_size(OVER)
    blocks = lax.axis_size(ACROSS)
    rows = kn // groups
    core = jnp.full((1,), lax.axis_index("core").astype(jnp.float32))
    over = jnp.full((1,), lax.axis_index(OVER), jnp.int32)
    spot = jnp.full((1,), lax.axis_index(ACROSS), jnp.int32)

    kinds = species.reshape(1, n)
    keep, give = factors(core, frac, kinds, feats, cot, miller, gain)
    pair = pair_of(keep, lax.ppermute(give, "core", SWAP))
    share = n // blocks * SHARED // 8
    pair, miller, some_frac, some_feats = lax.optimization_barrier((pair, miller, frac, feats))
    spread = across(pair.reshape(groups, rows, 2 * ch), OVER)
    weights, columns = prepare(miller, filter_weight, inv_n)
    some_frac = lax.dynamic_slice_in_dim(some_frac, spot[0] * share, share, axis=1)
    some_feats = lax.dynamic_slice_in_dim(some_feats, spot[0] * share, share, axis=0)
    spread, weights, some_frac, some_feats = lax.optimization_barrier((spread, weights, some_frac, some_feats))
    mine = across(panel_of(over, spread, weights), OVER).reshape(kn, 2 * ch)

    far = across(copies_of(core, mine, miller, ch, blocks), ACROSS)
    other = lax.ppermute(mine, "core", SWAP)
    scale = -TWO_PI / BOX * inv_k
    force = forces_of(core, frac, kinds, feats, cot, miller, gain, mine, other, columns, scale)
    far, force = lax.optimization_barrier((far, force))
    swapped = lax.ppermute(far, "core", SWAP)
    total, table = half_of(some_frac, far)
    part = share_of(total, table, swapped, some_feats, force, inv_k)
    part, frac = lax.optimization_barrier((part, frac))
    gathered = across(part, ACROSS)
    rest = rest_of(frac, feats, far, swapped, inv_k, share * blocks, TILE)
    gathered, rest = lax.optimization_barrier((gathered, rest))
    return tuple(finish(gathered, rest, share))


def solution(mesh):
    sizes = dict(mesh.shape)
    fine = Mesh(mesh.devices.reshape(2, sizes["dom"] // 4, 2, 2, sizes["ka"] // 2), ("xh", "z", "core", "xl", "y"))
    dom = ("xh", "z", "core")
    placed = (P(None, dom), P(dom), P(dom, None), P(dom, None), P(None, ("xl", "y")), P(), P())
    return jax.shard_map(
        body,
        mesh=fine,
        in_specs=placed,
        out_specs=(P(dom, None), P(None, dom)),
        check_vma=False,
    )
```

```python
import functools
import math

import jax
import jax.numpy as jnp
from jax import lax
from jax.experimental import pallas as pl
from jax.experimental.pallas import tpu as pltpu
from jax.sharding import Mesh, PartitionSpec as P

TWO_PI = 6.283185307179586
BOX = 64.0
MIB = 1024 * 1024
SINE = (4.4428679, -7.30744342, 3.59478803, -0.7843739)
OVER = ("xh", "z")
ACROSS = ("xl", "y")
SWAP = [(0, 1), (1, 0)]
DEPTH = 16
SHARED = 4
TILE = 1024
WHOLE = pl.BlockSpec(memory_space=pltpu.VMEM)
SCALAR = pl.BlockSpec(memory_space=pltpu.SMEM)
FAR = pl.BlockSpec(memory_space=pltpu.HBM)


def triple(x):
    hi = x.astype(jnp.bfloat16)
    rest = x - hi.astype(jnp.float32)
    mid = rest.astype(jnp.bfloat16)
    low = (rest - mid.astype(jnp.float32)).astype(jnp.bfloat16)
    return [hi, mid, low]


def places(frac):
    n = frac.shape[1]
    rest = DEPTH - 10
    return jnp.concatenate(
        triple(frac) + [jnp.ones((1, n), jnp.bfloat16), jnp.zeros((rest, n), jnp.bfloat16)], axis=0
    )


def contract(left, right, dims):
    return lax.dot_general(left, right, (dims, ((), ())), preferred_element_type=jnp.float32)


def cos_sin(turns):
    r = turns - jnp.round(turns)
    t = r * r
    s = (((SINE[3] * t + SINE[2]) * t + SINE[1]) * t + SINE[0]) * r
    square = s * s
    rest = 2.000004 - square
    return (1.0 - square).astype(jnp.bfloat16), (s * (rest * lax.rsqrt(rest))).astype(jnp.bfloat16)


def params(mib):
    return pltpu.CompilerParams(vmem_limit_bytes=mib * MIB)


def cost(flops, moved):
    return pl.CostEstimate(flops=flops, bytes_accessed=moved, transcendentals=0)


def steps_of(miller, core):
    kn = miller.shape[1]
    mills = miller.astype(jnp.float32) * (1.0 - 2.0 * core)
    rows = [mills, mills, mills, jnp.full((1, kn), 0.25 * core), jnp.zeros((DEPTH - 10, kn), jnp.float32)]
    return jnp.concatenate(rows, axis=0).astype(jnp.bfloat16)


def prepare_kernel(scale, miller, filter_weight, weights, columns):
    kn = miller.shape[1]
    column = jnp.concatenate([miller[...].astype(jnp.float32), jnp.zeros((5, kn), jnp.float32)], axis=0).T
    columns[...] = column
    length = jnp.sqrt(jnp.sum(column * column, axis=1, keepdims=True))
    count = filter_weight.shape[0]
    centres = lax.broadcasted_iota(jnp.int32, (1, count), 1).astype(jnp.float32) * (14.0 / (count - 1))
    basis = jnp.exp(-((length - centres) ** 2))
    weights[...] = scale * jnp.dot(
        basis, filter_weight[...], precision=lax.Precision.HIGHEST, preferred_element_type=jnp.float32
    )


def prepare(miller, filter_weight, scale):
    kn = miller.shape[1]
    return pl.pallas_call(
        functools.partial(prepare_kernel, scale),
        in_specs=[WHOLE, WHOLE],
        out_specs=[WHOLE] * 2,
        out_shape=[
            jax.ShapeDtypeStruct((kn, filter_weight.shape[1]), jnp.float32),
            jax.ShapeDtypeStruct((kn, 8), jnp.float32),
        ],
        compiler_params=params(4),
        cost_estimate=cost(10**6, 10**5),
        name="prepare",
    )(miller, filter_weight)


def embed(feats, species, gains3):
    kinds = gains3.shape[0] // 3
    onehot = (lax.broadcasted_iota(jnp.int32, (kinds, species.shape[1]), 0) == species).astype(jnp.float32)
    onehot = onehot.astype(jnp.bfloat16)
    gains = contract(jnp.concatenate([onehot, onehot, onehot], axis=0), gains3, ((0,), (0,)))
    return (feats.astype(jnp.float32) * gains).astype(jnp.bfloat16)


def factors_kernel(core, frac, species, feats, cot, miller, gain, keep, give, acc, held, tab):
    step = pl.program_id(0)
    kn = miller.shape[1]
    tile = frac.shape[1]

    @pl.when(step == 0)
    def _():
        acc[...] = jnp.zeros_like(acc)
        held[...] = steps_of(miller[...], core[0]).T

    place = places(frac[...])
    rows = embed(feats[...], species[...], jnp.concatenate(triple(gain[...]), axis=0))
    for at in range(0, tile, 256):
        c, s = cos_sin(contract(held[...], place[:, at:at + 256], ((1,), (0,))))
        tab[0:kn, at:at + 256] = c
        tab[kn:2 * kn, at:at + 256] = s
    both = jnp.concatenate([rows, cot[...]], axis=1)
    acc[...] += contract(tab[...], both, ((1,), (0,)))

    @pl.when(step == pl.num_programs(0) - 1)
    def _():
        keep[...] = acc[0:kn, :].astype(jnp.bfloat16)
        give[...] = acc[kn:2 * kn, :].astype(jnp.bfloat16)


def factors(core, frac, species, feats, cot, miller, gain, tile=2048):
    n, ch = feats.shape
    kn = miller.shape[1]
    return pl.pallas_call(
        factors_kernel,
        grid=(n // tile,),
        in_specs=[
            SCALAR,
            pl.BlockSpec((3, tile), lambda i: (0, i)),
            pl.BlockSpec((1, tile), lambda i: (0, i)),
            pl.BlockSpec((tile, ch), lambda i: (i, 0)),
            pl.BlockSpec((tile, ch), lambda i: (i, 0)),
            pl.BlockSpec(miller.shape, lambda i: (0, 0)),
            pl.BlockSpec(gain.shape, lambda i: (0, 0)),
        ],
        out_specs=[pl.BlockSpec((kn, 2 * ch), lambda i: (0, 0))] * 2,
        out_shape=[jax.ShapeDtypeStruct((kn, 2 * ch), jnp.bfloat16)] * 2,
        scratch_shapes=[
            pltpu.VMEM((2 * kn, 2 * ch), jnp.float32),
            pltpu.VMEM((kn, DEPTH), jnp.bfloat16),
            pltpu.VMEM((2 * kn, tile), jnp.bfloat16),
        ],
        compiler_params=params(58),
        cost_estimate=cost(8 * n * kn * ch, 8 * n * ch + 4 * n * kn),
        name="factors",
    )(core, frac, species, feats, cot, miller, gain)


def pair_kernel(keep, got, out):
    out[...] = (keep[...].astype(jnp.float32) + got[...].astype(jnp.float32)).astype(jnp.bfloat16)


def pair_of(keep, got):
    return pl.pallas_call(
        pair_kernel,
        in_specs=[WHOLE, WHOLE],
        out_specs=WHOLE,
        out_shape=jax.ShapeDtypeStruct(keep.shape, jnp.bfloat16),
        compiler_params=params(4),
        cost_estimate=cost(10**6, 10**4),
        name="pair",
    )(keep, got)


def panel_kernel(where, spread, weights, out):
    groups, rows, width = spread.shape
    total = spread[0].astype(jnp.float32)
    for i in range(1, groups):
        total += spread[i].astype(jnp.float32)
    w = weights[pl.ds(pl.multiple_of(where[0] * rows, rows), rows), :]
    panel = (total * jnp.concatenate([w] * (width // w.shape[1]), axis=1)).astype(jnp.bfloat16)
    for i in range(groups):
        out[i] = panel


def panel_of(where, spread, weights):
    return pl.pallas_call(
        panel_kernel,
        in_specs=[SCALAR, WHOLE, WHOLE],
        out_specs=WHOLE,
        out_shape=jax.ShapeDtypeStruct(spread.shape, jnp.bfloat16),
        compiler_params=params(4),
        cost_estimate=cost(10**6, 10**4),
        name="panel",
    )(where, spread, weights)


def send_all(block, out, sems):
    copies = [pltpu.make_async_copy(block, out.at[b], sems.at[b]) for b in range(out.shape[0])]
    for copy in copies:
        copy.start()
    for copy in copies:
        copy.wait()


def copies_kernel(core, mine, miller, out, block, sems):
    kn = miller.shape[1]
    block[0:kn, :] = mine[:, :block.shape[1]]
    block[kn:kn + DEPTH, :] = steps_of(miller[...], core[0])
    send_all(block, out, sems)


def copies_of(core, mine, miller, width, blocks):
    kn = miller.shape[1]
    return pl.pallas_call(
        copies_kernel,
        in_specs=[SCALAR, WHOLE, WHOLE],
        out_specs=FAR,
        out_shape=jax.ShapeDtypeStruct((blocks, kn + DEPTH, width), jnp.bfloat16),
        scratch_shapes=[
            pltpu.VMEM((kn + DEPTH, width), jnp.bfloat16),
            pltpu.SemaphoreType.DMA((blocks,)),
        ],
        compiler_params=params(6),
        cost_estimate=cost(10**6, 10**6),
        name="copies",
    )(core, mine, miller)


def forces_kernel(scale, core, frac, species, feats, cot, miller, gain, mine, other, columns, out, held, spread, rows):
    kn = columns.shape[0]
    tile = cot.shape[0]
    wide = spread.shape[2]
    steps = pl.num_programs(0)
    step = pl.program_id(0)
    each = tile // wide

    @pl.when(step == 0)
    def _():
        held[...] = steps_of(miller[...], core[0]).T
        for d in range(3):
            spread[d] = jnp.broadcast_to(columns[:, d:d + 1], spread.shape[1:])

    factor = (1.0 - 2.0 * core[0]) * scale
    place = places(frac[...])
    emb = embed(feats[...], species[...], jnp.concatenate(triple(gain[...]), axis=0))
    for j in range(each):
        at = j * wide
        both = jnp.concatenate([cot[at:at + wide, :], emb[at:at + wide, :]], axis=1)
        x = contract(mine[...], both, ((1,), (1,)))
        y = contract(other[...], both, ((1,), (1,)))
        c, s = cos_sin(contract(held[...], place[:, at:at + wide], ((1,), (0,))))
        grads = c.astype(jnp.float32) * y - s.astype(jnp.float32) * x
        for d in range(3):
            rows[pl.ds(d * each * steps + step * each + j, 1), :] = (
                jnp.sum(spread[d] * grads, axis=0, keepdims=True) * factor
            )

    @pl.when(step == steps - 1)
    def _():
        out[...] = rows[...].astype(jnp.bfloat16)


def forces_of(core, frac, species, feats, cot, miller, gain, mine, other, columns, scale, tile=1024):
    n, ch = cot.shape
    kn = columns.shape[0]
    count = 3 * n // ch
    return pl.pallas_call(
        functools.partial(forces_kernel, scale),
        grid=(n // tile,),
        in_specs=[
            SCALAR,
            pl.BlockSpec((3, tile), lambda i: (0, i)),
            pl.BlockSpec((1, tile), lambda i: (0, i)),
            pl.BlockSpec((tile, ch), lambda i: (i, 0)),
            pl.BlockSpec((tile, ch), lambda i: (i, 0)),
            pl.BlockSpec(miller.shape, lambda i: (0, 0)),
            pl.BlockSpec(gain.shape, lambda i: (0, 0)),
            pl.BlockSpec(mine.shape, lambda i: (0, 0)),
            pl.BlockSpec(other.shape, lambda i: (0, 0)),
            pl.BlockSpec(columns.shape, lambda i: (0, 0)),
        ],
        out_specs=pl.BlockSpec((count, ch), lambda i: (0, 0)),
        out_shape=jax.ShapeDtypeStruct((count, ch), jnp.bfloat16),
        scratch_shapes=[
            pltpu.VMEM((kn, DEPTH), jnp.bfloat16),
            pltpu.VMEM((3, kn, ch), jnp.float32),
            pltpu.VMEM((count, ch), jnp.float32),
        ],
        compiler_params=params(58),
        cost_estimate=cost(2000 * n * kn, 4 * n * kn + 4 * n * ch),
        name="forces",
    )(core, frac, species, feats, cot, miller, gain, mine, other, columns)


def finish_kernel(share, parts, rest, out, forces, sems):
    blocks, long, wide = parts.shape
    copies = [
        pltpu.make_async_copy(parts.at[b, pl.ds(0, share), :], out.at[pl.ds(b * share, share), :], sems.at[b])
        for b in range(blocks)
    ]
    for copy in copies:
        copy.start()
    count = long - share
    each = count // forces.shape[0]
    total = jnp.zeros((count, wide), jnp.float32)
    for b in range(blocks):
        total += parts[b, share:share + count, :].astype(jnp.float32)
    for d in range(forces.shape[0]):
        for j in range(each):
            forces[d:d + 1, j * wide:(j + 1) * wide] = total[d * each + j:d * each + j + 1, :]
    for copy in copies:
        copy.wait()


def finish(parts, rest, share):
    n, ch = rest.shape
    return pl.pallas_call(
        functools.partial(finish_kernel, share),
        in_specs=[WHOLE, FAR],
        out_specs=[FAR, WHOLE],
        out_shape=[jax.ShapeDtypeStruct((n, ch), jnp.bfloat16), jax.ShapeDtypeStruct((3, n), jnp.float32)],
        scratch_shapes=[pltpu.SemaphoreType.DMA((parts.shape[0],))],
        input_output_aliases={1: 0},
        compiler_params=params(8),
        cost_estimate=cost(10**6, 10**6),
        name="finish",
    )(parts, rest)


def half_kernel(frac, mine, total, table):
    kn = mine.shape[1] - DEPTH
    place = places(frac[...]).T
    sums = jnp.zeros(total.shape, jnp.float32)
    for b in range(mine.shape[0]):
        c, s = cos_sin(contract(place, mine[b, kn:kn + DEPTH, :], ((1,), (0,))))
        sums += contract(c, mine[b, 0:kn, :], ((1,), (0,)))
        table[:, b * kn:(b + 1) * kn] = s
    total[...] = sums


def half_of(frac, mine):
    n = frac.shape[1]
    blocks, long, ch = mine.shape
    return pl.pallas_call(
        half_kernel,
        in_specs=[WHOLE, WHOLE],
        out_specs=[WHOLE, WHOLE],
        out_shape=[
            jax.ShapeDtypeStruct((n, ch), jnp.float32),
            jax.ShapeDtypeStruct((n, blocks * (long - DEPTH)), jnp.bfloat16),
        ],
        compiler_params=params(8),
        cost_estimate=cost(2 * 10**9, 10**6),
        name="half",
    )(frac, mine)


def share_kernel(scale, total, table, other, feats, force, out, block, sems):
    kn = other.shape[1] - DEPTH
    share = feats.shape[0]
    sums = total[...]
    for b in range(other.shape[0]):
        sums += contract(table[:, b * kn:(b + 1) * kn], other[b, 0:kn, :], ((1,), (0,)))
    rows = (feats[...].astype(jnp.float32) + sums * scale).astype(jnp.bfloat16)
    block[0:share, :] = rows
    block[share:, :] = force[...]
    send_all(block, out, sems)


def share_of(total, table, other, feats, force, scale):
    share, ch = feats.shape
    return pl.pallas_call(
        functools.partial(share_kernel, scale),
        in_specs=[WHOLE] * 5,
        out_specs=FAR,
        out_shape=jax.ShapeDtypeStruct((other.shape[0], share + force.shape[0], ch), jnp.bfloat16),
        scratch_shapes=[
            pltpu.VMEM((share + force.shape[0], ch), jnp.bfloat16),
            pltpu.SemaphoreType.DMA((other.shape[0],)),
        ],
        compiler_params=params(8),
        cost_estimate=cost(10**9, 10**6),
        name="share",
    )(total, table, other, feats, force)


def rest_kernel(scale, frac, feats, mine, other, out):
    blocks = mine.shape[0]
    kn = mine.shape[1] - DEPTH
    rows = 256
    place = places(frac[...]).T
    panels = [jnp.concatenate([p[b, 0:kn, :] for b in range(blocks)], axis=0) for p in (mine, other)]

    def tables_at(at):
        pairs = [
            cos_sin(contract(place[at:at + rows], mine[b, kn:kn + DEPTH, :], ((1,), (0,)))) for b in range(blocks)
        ]
        return [jnp.concatenate(table, axis=1) for table in zip(*pairs)]

    after = tables_at(0)
    for at in range(0, feats.shape[0], rows):
        here = slice(at, at + rows)
        first, second = after
        if at + rows < feats.shape[0]:
            after = tables_at(at + rows)
        total = contract(first, panels[0], ((1,), (0,))) + contract(second, panels[1], ((1,), (0,)))
        out[here, :] = (feats[here, :].astype(jnp.float32) + total * scale).astype(jnp.bfloat16)


def rest_of(frac, feats, mine, other, scale, start, tile):
    n, ch = feats.shape
    first = start // tile
    return pl.pallas_call(
        functools.partial(rest_kernel, scale),
        grid=((n - start) // tile,),
        in_specs=[
            pl.BlockSpec((3, tile), lambda i: (0, first + i)),
            pl.BlockSpec((tile, ch), lambda i: (first + i, 0)),
            pl.BlockSpec(mine.shape, lambda i: (0, 0, 0)),
            pl.BlockSpec(other.shape, lambda i: (0, 0, 0)),
        ],
        out_specs=pl.BlockSpec((tile, ch), lambda i: (first + i, 0)),
        out_shape=jax.ShapeDtypeStruct((n, ch), jnp.bfloat16),
        compiler_params=params(58),
        cost_estimate=cost(10**10, 10**6),
        name="rest",
    )(frac, feats, mine, other)


def across(x, axes):
    return lax.all_to_all(x, axes, 0, 0)


def body(frac, species, feats, cot, miller, gain, filter_weight):
    n, ch = feats.shape
    kn = miller.shape[1]
    inv_n = 1.0 / math.sqrt(n * lax.axis_size(("xh", "z", "core")))
    inv_k = 1.0 / math.sqrt(kn * lax.axis_size(ACROSS))
    groups = lax.axis_size(OVER)
    blocks = lax.axis_size(ACROSS)
    rows = kn // groups
    core = jnp.full((1,), lax.axis_index("core").astype(jnp.float32))
    over = jnp.full((1,), lax.axis_index(OVER), jnp.int32)
    spot = jnp.full((1,), lax.axis_index(ACROSS), jnp.int32)

    kinds = species.reshape(1, n)
    keep, give = factors(core, frac, kinds, feats, cot, miller, gain)
    pair = pair_of(keep, lax.ppermute(give, "core", SWAP))
    share = n // blocks * SHARED // 8
    pair, miller, some_frac, some_feats = lax.optimization_barrier((pair, miller, frac, feats))
    spread = across(pair.reshape(groups, rows, 2 * ch), OVER)
    weights, columns = prepare(miller, filter_weight, inv_n)
    some_frac = lax.dynamic_slice_in_dim(some_frac, spot[0] * share, share, axis=1)
    some_feats = lax.dynamic_slice_in_dim(some_feats, spot[0] * share, share, axis=0)
    spread, weights, some_frac, some_feats = lax.optimization_barrier((spread, weights, some_frac, some_feats))
    mine = across(panel_of(over, spread, weights), OVER).reshape(kn, 2 * ch)

    far = across(copies_of(core, mine, miller, ch, blocks), ACROSS)
    other = lax.ppermute(mine, "core", SWAP)
    scale = -TWO_PI / BOX * inv_k
    force = forces_of(core, frac, kinds, feats, cot, miller, gain, mine, other, columns, scale)
    far, force = lax.optimization_barrier((far, force))
    swapped = lax.ppermute(far, "core", SWAP)
    total, table = half_of(some_frac, far)
    part = share_of(total, table, swapped, some_feats, force, inv_k)
    part, frac = lax.optimization_barrier((part, frac))
    gathered = across(part, ACROSS)
    rest = rest_of(frac, feats, far, swapped, inv_k, share * blocks, TILE)
    gathered, rest = lax.optimization_barrier((gathered, rest))
    return tuple(finish(gathered, rest, share))


def solution(mesh):
    sizes = dict(mesh.shape)
    fine = Mesh(mesh.devices.reshape(2, sizes["dom"] // 4, 2, 2, sizes["ka"] // 2), ("xh", "z", "core", "xl", "y"))
    dom = ("xh", "z", "core")
    placed = (P(None, dom), P(dom), P(dom, None), P(dom, None), P(None, ("xl", "y")), P(), P())
    return jax.shard_map(
        body,
        mesh=fine,
        in_specs=placed,
        out_specs=(P(dom, None), P(None, dom)),
        check_vma=False,
    )
```
